32 devices in a mesh: wide: 8 (over z, y), narrow: 4 (over x, core).
Axes of the slice: x: 2, y: 2, z: 4, core: 2. Of those that a mesh axis runs over, the one named last changes fastest.
Arguments:
- loads: float32 [3, 256, 128, 128], P(None, 'wide', 'narrow'), may hold values from -48 to 48
- targets: float32 [3, 256, 128, 128], P(None, 'wide', 'narrow'), may hold values from -48 to 48
- stiffness: float32 [256, 128, 128], P('wide', 'narrow'), may hold values from 0.5 to 2
- tile_state: int32 [8, 4], P('wide', 'narrow'), may hold values from 0 to 2, as said below
- design_order: int32 [32], replicated, may hold values from 0 to 31, each once
Outputs:
- displacement: float32 [3, 256, 128, 128], P(None, 'wide', 'narrow')
- adjoint: float32 [3, 256, 128, 128], P(None, 'wide', 'narrow')
- design_sens: float32 [32], P(('wide', 'narrow'))
The draws below stay inside these ranges and needn't reach their ends.
Inputs may be any that keep to these rules, and one draw needn't show every extreme that they name: `tile_state`: 0 marks a tile without rock, 1 rock, 2 weak backfill. `design_order`: each design cell once.
All inputs are finite; a program needn't handle non-finite values.
Results may differ from the reference program's by a relative error of at most 0.0003.
Values sent between devices are 32-bit elements; how exact they have to be, the bound alone decides.
A program may use at most 128 MiB of HBM per device.

```python
import math
import jax
import jax.numpy as jnp
from jax import lax

TPX = 1
TPY = 1
BX = 32
BY = 32
BZ = 128
DZ = 4
SWEEPS = 3
GX = 8
GY = 4
NX = 256
NY = 128
DESIGN = 32


def draw_tile_state(key, part):
    key = jax.random.fold_in(key, 11)
    level_key, roll_key, weak_key = jax.random.split(key, 3)
    level = jax.random.randint(level_key, (GX // TPX, GY // TPY), 1, 5)
    level_tiles = jnp.repeat(jnp.repeat(level, TPX, 0), TPY, 1)
    roll = jax.random.randint(roll_key, (GX, GY), 0, 4)
    weak = jax.random.randint(weak_key, (GX, GY), 0, 4) == 0
    state = jnp.where(roll < level_tiles, jnp.where(weak, 2, 1), 0)
    return state.astype(jnp.int32)


def steps_of(key, shape, pieces, least, high):
    level = 1.0
    for axis_at, shards_of in pieces:
        heights = jax.random.uniform(jax.random.fold_in(jax.random.fold_in(key, 6), axis_at), (shards_of,), jnp.float32, least / len(pieces), high / len(pieces))
        level = level * jnp.repeat(jnp.exp(heights), shape[axis_at] // shards_of).reshape((-1,) + (1,) * (len(shape) - 1 - axis_at))
    return level


def noise(own_key, extent, scale, reach, cuts=(), held_as=jnp.bfloat16):
    array = jax.random.normal(own_key, extent, jnp.float32) * scale
    if len(cuts) > 0:
        array = steps_of(own_key, extent, cuts, -0.22, 0.18) * array
    return jnp.clip(array, min=-reach, max=reach).astype(held_as)


def setup_inputs(seed: int = 0) -> dict:
    keys = jax.random.split(jax.random.key(seed), 6)
    return {
        "loads": noise(keys[0], (3, NX, NY, BZ), 8.0, 48.0, ((1, 8), (2, 4)), jnp.float32),
        "targets": noise(keys[1], (3, NX, NY, BZ), 8.0, 48.0, ((1, 8), (2, 4)), jnp.float32),
        "stiffness": jnp.clip(jnp.exp(math.log(2.0) - 1.3862944 * jax.random.uniform(keys[2], (NX, NY, BZ), jnp.float32) ** steps_of(keys[2], (NX, NY, BZ), ((0, 8), (1, 4)), -0.2, 0.2)), 0.5, 2.0),
        "tile_state": draw_tile_state(jax.random.fold_in(keys[5], 71), 0),
        "design_order": jax.random.permutation(keys[4], DESIGN).astype(jnp.int32),
    }


MASS_SHIFT = 0.5
WEAK_FILL = 0.25
LOW_BOUND = 0.0625
HIGH_BOUND = 34.0
AXES_OF = (0, 0, 1, 1, 2, 2)

def chebyshev_weights(sweeps):
    center = 0.5 * (HIGH_BOUND + LOW_BOUND)
    spread = 0.5 * (HIGH_BOUND - LOW_BOUND)
    bound_ratio = center / spread
    previous = 1.0 / bound_ratio
    weights = []
    for sweep_index in range(sweeps):
        current = 1.0 / (2.0 * bound_ratio - previous)
        weights.append((current * previous, 2.0 * current / spread))
        previous = current
    return (center, weights)

def axis_gain(axis):
    return jnp.asarray([2.0 if component == axis else 1.0 for component in range(3)], jnp.float32).reshape(3, 1, 1, 1)

def neighbours(padded):
    return [padded[..., :-2, 1:-1, 1:-1], padded[..., 2:, 1:-1, 1:-1], padded[..., 1:-1, :-2, 1:-1], padded[..., 1:-1, 2:, 1:-1], padded[..., 1:-1, 1:-1, :-2], padded[..., 1:-1, 1:-1, 2:]]

def face_terms(stiff_padded):
    center = stiff_padded[1:-1, 1:-1, 1:-1]
    faces = []
    shares = []
    for other in neighbours(stiff_padded):
        present = other > 0.0
        faces.append(jnp.where(present, 0.5 * (center + other), center))
        shares.append(jnp.where(present, 0.5, 1.0).astype(jnp.float32))
    return (faces, shares)

def apply_operator(padded, cell_stiff, active, faces):
    center_field = padded[..., 1:-1, 1:-1, 1:-1]
    total = MASS_SHIFT * cell_stiff * center_field
    for direction, (other, face) in enumerate(zip(neighbours(padded), faces)):
        total = total + axis_gain(AXES_OF[direction]) * face * (center_field - other)
    return active * total

def pad_space(field):
    return jnp.pad(field, ((0, 0), (1, 1), (1, 1), (1, 1)))

def cell_partials(upper, lower, cell_stiff, active, shares):
    center_u = upper[..., 1:-1, 1:-1, 1:-1]
    center_l = lower[..., 1:-1, 1:-1, 1:-1]
    total = MASS_SHIFT * center_u * center_l
    for direction, (other_u, other_l, share) in enumerate(zip(neighbours(upper), neighbours(lower), shares)):
        total = total + axis_gain(AXES_OF[direction]) * share * (center_u - other_u) * (center_l - other_l)
    return -active * cell_stiff * lax.optimization_barrier(jnp.sum(total, axis=0))

def solve_field(source, cell_stiff, active, faces):
    center, weights = chebyshev_weights(SWEEPS)
    field = jnp.zeros_like(source)
    residual = source
    direction = source / center
    for sweep_index in range(SWEEPS):
        image = apply_operator(pad_space(direction), cell_stiff, active, faces)
        field = field + direction
        if sweep_index + 1 < SWEEPS:
            residual = residual - image
            direction = weights[sweep_index][0] * direction + weights[sweep_index][1] * residual
    return field

def reference(loads, targets, stiffness, tile_state, design_order):
    factor = jnp.where(tile_state == 1, 1.0, jnp.where(tile_state == 2, WEAK_FILL, 0.0)).astype(jnp.float32)
    cell_factor = jnp.repeat(jnp.repeat(factor, BX, 0), BY, 1)[:, :, None]
    cell_stiff = stiffness * cell_factor
    active = (cell_factor > 0.0).astype(jnp.float32)
    faces, shares = face_terms(jnp.pad(cell_stiff, 1))
    displacement = solve_field(active * loads, cell_stiff, active, faces)
    adjoint = solve_field(active * targets, cell_stiff, active, faces)
    partial_value = cell_partials(pad_space(displacement), pad_space(adjoint), cell_stiff, active, shares)
    blocks = partial_value.reshape(GX // 2, 2 * BX, GY // 2, 2 * BY, DZ, BZ // DZ).sum(axis=(1, 3, 5))
    scale = math.sqrt(4 * BX * BY * (BZ // DZ))
    group = blocks.reshape(-1) / scale
    return (displacement, adjoint, group[design_order.astype(jnp.int32)])
```

```python
import functools
import math

import jax
import jax.numpy as jnp
from jax import lax
from jax.experimental import pallas as pl
from jax.experimental.pallas import tpu as pltpu
from jax.sharding import PartitionSpec as P

DZ = 4
SWEEPS = 3
WEAK_FILL = 0.25
LOW_BOUND = 0.0625
HIGH_BOUND = 34.0
F32 = jnp.float32


def chebyshev_weights(sweeps):
    center = 0.5 * (HIGH_BOUND + LOW_BOUND)
    spread = 0.5 * (HIGH_BOUND - LOW_BOUND)
    bound_ratio = center / spread
    previous = 1.0 / bound_ratio
    weights = []
    for sweep_index in range(sweeps):
        current = 1.0 / (2.0 * bound_ratio - previous)
        weights.append((current * previous, 2.0 * current / spread))
        previous = current
    return (center, weights)


def sweep_constants():
    center, weights = chebyshev_weights(SWEEPS)
    (w00, w01), (w10, w11) = weights[0], weights[1]
    alpha = w00 / center + w01
    beta = w01 / center
    p = 1.0 / center - w11 * w00 / (w01 * center)
    q = 1.0 + w10 + w11 / w01
    return alpha, beta, p, q, w11


def kernel(
    nw, nn, loads, targets, stiff, state, order, u_out, l_out, sens,
    s, d, kh, fac_own, fac_in, ys_out, ys_in, yd_out, yd_in, yx_out, yx_in,
    tile_a, send_a, tile_b, send_b,
    in_sem, out_sem, xs_send, xs_recv, ys_send, ys_recv, xd_send, xd_recv,
    yd_send, yd_recv, xx_send, xx_recv, a_send, a_recv, b_send, b_recv,
):
    cells_x, cells_y, depth = stiff.shape
    last = cells_x + 1
    w = lax.axis_index("wide")
    n = lax.axis_index("narrow")
    has_x = (w > 0, w < nw - 1)
    has_y = (n > 0, n < nn - 1)
    steps = (-1, 1)

    def at(wi, ni):
        return dict(device_id=(wi, ni), device_id_type=pl.DeviceIdType.MESH)

    def x_peer(side):
        return at(w + steps[side], n)

    def y_peer(side):
        return at(w, n + steps[side])

    barrier = pltpu.get_barrier_semaphore()
    for m in range(nn):
        @pl.when(m != n)
        def _():
            pl.semaphore_signal(barrier, inc=1, **at(w, jnp.int32(m)))
    for m in range(nw):
        @pl.when(m != w)
        def _():
            pl.semaphore_signal(barrier, inc=1, **at(jnp.int32(m), n))

    local = [
        pltpu.make_async_copy(stiff, kh.at[pl.ds(1, cells_x)], in_sem.at[0]),
        pltpu.make_async_copy(loads, s.at[pl.ds(0, 3), pl.ds(1, cells_x)], in_sem.at[1]),
        pltpu.make_async_copy(targets, s.at[pl.ds(3, 3), pl.ds(1, cells_x)], in_sem.at[2]),
    ]
    for copy in local:
        copy.start()

    own_state = state[0, 0]
    factor = jnp.where(own_state == 1, 1.0, jnp.where(own_state == 2, WEAK_FILL, 0.0)).astype(F32)
    act = jnp.where(factor > 0.0, 1.0, 0.0).astype(F32)
    fac_own[...] = jnp.full(fac_own.shape, factor, F32)

    pl.semaphore_wait(barrier, nn - 1 + nw - 1)

    edge = (0, cells_x - 1)
    ghost = (0, last)

    def xs_copies(side):
        there = 1 - side
        pairs = (
            (stiff.at[edge[side]], kh.at[ghost[there]]),
            (loads.at[:, edge[side]], s.at[pl.ds(0, 3), ghost[there]]),
            (targets.at[:, edge[side]], s.at[pl.ds(3, 3), ghost[there]]),
            (fac_own, fac_in.at[there]),
        )
        return [
            pltpu.make_async_remote_copy(
                src_ref=a, dst_ref=b, send_sem=xs_send.at[side, t], recv_sem=xs_recv.at[there, t],
                **x_peer(side))
            for t, (a, b) in enumerate(pairs)
        ]

    def one(src, dst, sends, recvs, side, peer):
        return pltpu.make_async_remote_copy(
            src_ref=src, dst_ref=dst, send_sem=sends.at[side], recv_sem=recvs.at[1 - side],
            **peer(side))

    def ys_copy(side):
        return one(ys_out.at[side], ys_in.at[1 - side], ys_send, ys_recv, side, y_peer)

    def yd_copy(side):
        return one(yd_out.at[side], yd_in.at[1 - side], yd_send, yd_recv, side, y_peer)

    def xd_copy(side):
        return one(d.at[:, 1 + edge[side]], d.at[:, ghost[1 - side]], xd_send, xd_recv, side, x_peer)

    def xx_copy():
        return pltpu.make_async_remote_copy(
            src_ref=s.at[:, cells_x], dst_ref=s.at[:, 0], send_sem=xx_send.at[0],
            recv_sem=xx_recv.at[0], **x_peer(1))

    def yx_copy():
        return pltpu.make_async_remote_copy(
            src_ref=yx_out, dst_ref=yx_in, send_sem=xx_send.at[1],
            recv_sem=xx_recv.at[1], **y_peer(1))

    for side in (0, 1):
        @pl.when(has_x[side])
        def _():
            for copy in xs_copies(side):
                copy.start()

        @pl.when(jnp.logical_not(has_x[side]))
        def _():
            s[:, ghost[side]] = jnp.zeros((6, cells_y, depth), F32)
            d[:, ghost[side]] = jnp.zeros((6, cells_y, depth), F32)
            fac_in[side] = jnp.zeros(fac_in.shape[1:], F32)

        @pl.when(jnp.logical_not(has_y[side]))
        def _():
            ys_in[side] = jnp.zeros(ys_in.shape[1:], F32)
            yd_in[side] = jnp.zeros(yd_in.shape[1:], F32)

    @pl.when(n == 0)
    def _():
        yx_in[...] = jnp.zeros(yx_in.shape, F32)

    for copy in local:
        copy.wait()

    half_factor = 0.5 * factor
    y_edge = (slice(0, 1), slice(cells_y - 1, cells_y))

    def prepare(t, carry):
        plane = kh[t + 1] * half_factor
        kh[t + 1] = plane
        for side in (0, 1):
            ys_out[side, 6, pl.ds(t, 1)] = plane[y_edge[side]]
            for c in range(6):
                ys_out[side, c, pl.ds(t, 1)] = s[c, t + 1, y_edge[side]] * act
        return carry

    lax.fori_loop(0, cells_x, prepare, 0)

    for side in (0, 1):
        @pl.when(has_y[side])
        def _():
            ys_copy(side).start()

    for side in (0, 1):
        @pl.when(has_y[side])
        def _():
            ys_copy(1 - side).wait_recv()

    row = lax.broadcasted_iota(jnp.int32, (cells_y, depth), 0)
    lane = lax.broadcasted_iota(jnp.int32, (cells_y, depth), 1)
    first_row, last_row = row == 0, row == cells_y - 1
    first_lane, last_lane = lane == 0, lane == depth - 1

    def down(v, halo):
        return jnp.where(first_row, halo, pltpu.roll(v, 1, 0))

    def up(v, halo):
        return jnp.where(last_row, halo, pltpu.roll(v, cells_y - 1, 0))

    def left(v):
        return pltpu.roll(v, 1, 1)

    def right(v):
        return pltpu.roll(v, depth - 1, 1)

    def y_stiff(kc, side, t):
        halo = ys_in[side, 6, pl.ds(t, 1)]
        return jnp.where(halo > 0.0, halo, kc[y_edge[side]])

    def operator(src, y_in, i, emit):
        t = i - 1
        kc = kh[i]
        fxm, fxp = kc + kh[i - 1], kc + kh[i + 1]
        fym = kc + down(kc, y_stiff(kc, 0, t))
        fyp = kc + up(kc, y_stiff(kc, 1, t))
        fzm = kc + jnp.where(first_lane, kc, left(kc))
        fzp = kc + jnp.where(last_lane, kc, right(kc))
        sums = (fxm + fxp, fym + fyp, fzm + fzp)
        total = kc + (sums[0] + sums[1] + sums[2])
        diag = [total + part for part in sums]
        fzm = jnp.where(first_lane, 0.0, fzm)
        fzp = jnp.where(last_lane, 0.0, fzp)
        for c in range(6):
            v = src[c, i]
            ax = fxm * src[c, i - 1] + fxp * src[c, i + 1]
            ay = fym * down(v, y_in[0, c, pl.ds(t, 1)]) + fyp * up(v, y_in[1, c, pl.ds(t, 1)])
            az = fzm * left(v) + fzp * right(v)
            mine = (ax, ay, az)[c % 3]
            emit(c, i, v, diag[c % 3] * v - ((ax + ay) + (az + mine)))

    alpha, beta, p, q, wd = sweep_constants()
    alpha_a, beta_a, p_a, wd_a = alpha * act, beta * act, p * act, wd * act

    def emit_d(c, i, v, image):
        plane = alpha_a * v - beta_a * image
        d[c, i] = plane
        for side in (0, 1):
            yd_out[side, c, pl.ds(i - 1, 1)] = plane[y_edge[side]]

    def emit_x(c, i, v, image):
        plane = p_a * s[c, i] + (q * v - wd_a * image)
        s[c, i] = plane
        yx_out[c, pl.ds(i - 1, 1)] = plane[y_edge[1]]

    def first_pass(i, carry):
        operator(s, ys_in, i, emit_d)
        return carry

    def second_pass(i, carry):
        operator(d, yd_in, i, emit_x)
        return carry

    lax.fori_loop(2, cells_x, first_pass, 0)

    for side in (0, 1):
        @pl.when(has_x[side])
        def _():
            for copy in xs_copies(1 - side):
                copy.wait_recv()
        theirs = fac_in[side][0:1]
        present = theirs > 0.0
        inner = kh[1 + edge[side]]

        @pl.when(has_x[side])
        def _():
            kh[ghost[side]] = jnp.where(present, kh[ghost[side]] * (0.5 * theirs), inner)
            for c in range(6):
                s[c, ghost[side]] = jnp.where(present, s[c, ghost[side]], 0.0)

        @pl.when(jnp.logical_not(has_x[side]))
        def _():
            kh[ghost[side]] = inner

    lax.fori_loop(0, 2, lambda t, c: first_pass(1 + t * (cells_x - 1), c), 0)

    for side in (0, 1):
        @pl.when(has_x[side])
        def _():
            xd_copy(side).start()

    for side in (0, 1):
        @pl.when(has_y[side])
        def _():
            yd_copy(side).start()

    for side in (0, 1):
        @pl.when(has_y[side])
        def _():
            yd_copy(1 - side).wait_recv()

    lax.fori_loop(2, cells_x, second_pass, 0)

    for side in (0, 1):
        @pl.when(has_x[side])
        def _():
            xd_copy(1 - side).wait_recv()

    lax.fori_loop(0, 2, lambda t, c: second_pass(1 + (1 - t) * (cells_x - 1), c), 0)

    @pl.when(has_x[1])
    def _():
        xx_copy().start()

    @pl.when(has_y[1])
    def _():
        yx_copy().start()

    results = [
        pltpu.make_async_copy(s.at[pl.ds(0, 3), pl.ds(1, cells_x)], u_out, out_sem.at[0]),
        pltpu.make_async_copy(s.at[pl.ds(3, 3), pl.ds(1, cells_x)], l_out, out_sem.at[1]),
    ]
    for copy in results:
        copy.start()

    @pl.when(has_y[0])
    def _():
        yx_copy().wait_recv()

    other_share = jnp.where(factor > 0.0, 1.0, 2.0).astype(F32)
    end_x = jnp.where(w == nw - 1, 2.0, 0.0).astype(F32)
    end_y = jnp.where(n == nn - 1, 2.0, 0.0).astype(F32)
    zero_plane = jnp.zeros((cells_y, depth), F32)
    zero_row = jnp.zeros((1, depth), F32)

    def products(shift, axis):
        total = None
        for c in range(3):
            (u, un), (l, ln) = shift(c), shift(c + 3)
            term = (u - un) * (l - ln)
            if c == axis:
                term = term + term
            total = term if total is None else total + term
        return total

    def face_sums(t, carry, behind=True):
        own, back, below = carry
        i = t + 1
        kc = kh[i]
        fields = [s[c, i] for c in range(6)]
        squares = [fields[c] * fields[c + 3] for c in range(3)]
        mass = squares[0] + squares[1] + squares[2]
        far_x = jnp.where(t == cells_x - 1, end_x, 0.0)
        far_y = jnp.where(last_row, end_y, 0.0)
        far_z = jnp.where(last_lane, 2.0, 0.0)
        own = own + kc * (
            mass + far_x * (mass + squares[0]) + far_y * (mass + squares[1])
            + far_z * (mass + squares[2]))
        if behind:
            px = products(lambda c: (fields[c], s[c, i - 1]), 0)
            own = own + (kc + kh[i - 1]) * px
        halo = ys_in[0, 6, pl.ds(t, 1)]
        py = products(lambda c: (fields[c], down(fields[c], yx_in[c, pl.ds(t, 1)])), 1)
        edge_weight = jnp.where(halo > 0.0, 0.0, kc[0:1])
        own = own + (kc + down(kc, edge_weight)) * py
        below = below + (other_share * halo) * py[0:1]
        pz = products(lambda c: (fields[c], jnp.where(first_lane, 0.0, left(fields[c]))), 2)
        own = own + jnp.where(first_lane, kc + kc, kc) * pz
        back = back + jnp.where(first_lane, 0.0, left(kc)) * pz
        return own, back, below

    start = face_sums(0, (zero_plane, zero_plane, zero_row), behind=False)
    own, back, below = lax.fori_loop(1, cells_x, face_sums, start)

    @pl.when(has_x[0])
    def _():
        xx_copy().wait_recv()

    px = products(lambda c: (s[c, 1], s[c, 0]), 0)
    present = fac_in[0][0:1] > 0.0
    own = own + kh[1] * jnp.where(present, 1.0, 2.0) * px
    beside = jnp.where(present, other_share * kh[0], 0.0) * px

    def fold(v):
        return jnp.sum(v, axis=0, keepdims=True)

    own_row = fold(own) + right(jnp.broadcast_to(fold(back), (8, depth)))[0:1]
    send_a[...] = jnp.concatenate(
        [own_row, fold(beside), below, jnp.zeros((5, depth), F32)], axis=0)

    def a_copy(m, slot):
        return pltpu.make_async_remote_copy(
            src_ref=send_a, dst_ref=tile_a.at[slot], send_sem=a_send.at[m],
            recv_sem=a_recv.at[slot], **at(w, jnp.int32(m)))

    def b_copy(m, slot):
        return pltpu.make_async_remote_copy(
            src_ref=send_b, dst_ref=tile_b.at[slot], send_sem=b_send.at[m],
            recv_sem=b_recv.at[slot], **at(jnp.int32(m), n))

    for m in range(nn):
        @pl.when(m != n)
        def _():
            a_copy(m, n).start()
    tile_a[n] = send_a[...]
    for m in range(nn):
        @pl.when(m != n)
        def _():
            a_copy(m, m).wait_recv()

    groups_y = nn // 2
    rows = [zero_row] * (2 * groups_y)
    for m in range(nn):
        tile = tile_a[m]
        rows[m // 2] = rows[m // 2] + tile[0:1]
        rows[groups_y + m // 2] = rows[groups_y + m // 2] + tile[1:2]
        if m > 0:
            rows[(m - 1) // 2] = rows[(m - 1) // 2] + tile[2:3]
    high = send_b.shape[0]
    if high > len(rows):
        rows.append(jnp.zeros((high - len(rows), depth), F32))
    send_b[...] = jnp.concatenate(rows, axis=0)

    for m in range(nw):
        @pl.when(m != w)
        def _():
            b_copy(m, w).start()
    tile_b[w] = send_b[...]
    for m in range(nw):
        @pl.when(m != w)
        def _():
            b_copy(m, m).wait_recv()

    wanted = order[w * nn + n]
    b_row = lax.broadcasted_iota(jnp.int32, (high, depth), 0)
    b_block = lax.broadcasted_iota(jnp.int32, (high, depth), 1) // (depth // DZ)
    picked = jnp.zeros((high, depth), F32)
    for m in range(nw):
        near = ((m // 2) * groups_y + b_row) * DZ + b_block
        far = (((m - 1) // 2) * groups_y + b_row - groups_y) * DZ + b_block if m > 0 else -1
        index = jnp.where(b_row < groups_y, near, far)
        index = jnp.where(b_row < 2 * groups_y, index, -1)
        picked = picked + jnp.where(index == wanted, tile_b[m], 0.0)
    scale = math.sqrt(4 * cells_x * cells_y * (depth // DZ))
    sens[0] = jnp.sum(picked) * (-1.0 / scale)

    for copy in results:
        copy.wait()
    for side in (0, 1):
        @pl.when(has_x[side])
        def _():
            for copy in xs_copies(side):
                copy.wait_send()
            xd_copy(side).wait_send()

        @pl.when(has_y[side])
        def _():
            ys_copy(side).wait_send()
            yd_copy(side).wait_send()

    @pl.when(has_x[1])
    def _():
        xx_copy().wait_send()

    @pl.when(has_y[1])
    def _():
        yx_copy().wait_send()

    for m in range(nn):
        @pl.when(m != n)
        def _():
            a_copy(m, n).wait_send()
    for m in range(nw):
        @pl.when(m != w)
        def _():
            b_copy(m, w).wait_send()


def body(nw, nn, loads, targets, stiffness, tile_state, design_order):
    cells_x, cells_y, depth = stiffness.shape
    high = -(-nn // 8) * 8
    dma = pltpu.SemaphoreType.DMA
    vmem = pltpu.VMEM
    anywhere = pl.BlockSpec(memory_space=pl.ANY)
    smem = pl.BlockSpec(memory_space=pltpu.SMEM)
    field = (6, cells_x + 2, cells_y, depth)
    return pl.pallas_call(
        functools.partial(kernel, nw, nn),
        out_shape=(
            jax.ShapeDtypeStruct(loads.shape, F32),
            jax.ShapeDtypeStruct(targets.shape, F32),
            jax.ShapeDtypeStruct((1,), F32),
        ),
        in_specs=[anywhere, anywhere, anywhere, smem, smem],
        out_specs=(anywhere, anywhere, smem),
        scratch_shapes=[
            vmem(field, F32),
            vmem(field, F32),
            vmem(field[1:], F32),
            vmem((8, depth), F32),
            vmem((2, 8, depth), F32),
            vmem((2, 7, cells_x, depth), F32),
            vmem((2, 7, cells_x, depth), F32),
            vmem((2, 6, cells_x, depth), F32),
            vmem((2, 6, cells_x, depth), F32),
            vmem((6, cells_x, depth), F32),
            vmem((6, cells_x, depth), F32),
            vmem((nn, 8, depth), F32),
            vmem((8, depth), F32),
            vmem((nw, high, depth), F32),
            vmem((high, depth), F32),
            dma((3,)),
            dma((2,)),
            dma((2, 4)),
            dma((2, 4)),
            dma((2,)),
            dma((2,)),
            dma((2,)),
            dma((2,)),
            dma((2,)),
            dma((2,)),
            dma((2,)),
            dma((2,)),
            dma((nn,)),
            dma((nn,)),
            dma((nw,)),
            dma((nw,)),
        ],
        compiler_params=pltpu.CompilerParams(
            collective_id=0, has_side_effects=True, vmem_limit_bytes=40 * 1024 * 1024
        ),
    )(loads, targets, stiffness, tile_state, design_order)


def solution(mesh):
    placed = (
        P(None, "wide", "narrow", None),
        P(None, "wide", "narrow", None),
        P("wide", "narrow", None),
        P("wide", "narrow"),
        P(),
    )
    return jax.shard_map(
        functools.partial(body, mesh.shape["wide"], mesh.shape["narrow"]),
        mesh=mesh,
        in_specs=placed,
        out_specs=(
            P(None, "wide", "narrow", None),
            P(None, "wide", "narrow", None),
            P(("wide", "narrow")),
        ),
        check_vma=False,
    )
```

```python
import functools
import math

import jax
import jax.numpy as jnp
from jax import lax
from jax.experimental import pallas as pl
from jax.experimental.pallas import tpu as pltpu
from jax.sharding import PartitionSpec as P

DZ = 4
SWEEPS = 3
WEAK_FILL = 0.25
LOW_BOUND = 0.0625
HIGH_BOUND = 34.0
F32 = jnp.float32


def chebyshev_weights(sweeps):
    center = 0.5 * (HIGH_BOUND + LOW_BOUND)
    spread = 0.5 * (HIGH_BOUND - LOW_BOUND)
    bound_ratio = center / spread
    previous = 1.0 / bound_ratio
    weights = []
    for sweep_index in range(sweeps):
        current = 1.0 / (2.0 * bound_ratio - previous)
        weights.append((current * previous, 2.0 * current / spread))
        previous = current
    return (center, weights)


def sweep_constants():
    center, weights = chebyshev_weights(SWEEPS)
    (w00, w01), (w10, w11) = weights[0], weights[1]
    alpha = w00 / center + w01
    beta = w01 / center
    p = 1.0 / center - w11 * w00 / (w01 * center)
    q = 1.0 + w10 + w11 / w01
    return alpha, beta, p, q, w11


def kernel(
    nw, nn, loads, targets, stiff, state, order, s, sens,
    d, kh, fac_own, fac_in, ys_out, ys_in, yd_out, yd_in, yx_out, yx_in,
    tile_a, send_a,
    in_sem, xs_send, xs_recv, ys_send, ys_recv, xd_send, xd_recv,
    yd_send, yd_recv, xx_send, xx_recv, a_send, a_recv,
):
    cells_x, cells_y, depth = stiff.shape
    last = cells_x + 1
    w = lax.axis_index("wide")
    n = lax.axis_index("narrow")
    has_x = (w > 0, w < nw - 1)
    has_y = (n > 0, n < nn - 1)
    steps = (-1, 1)

    def at(wi, ni):
        return dict(device_id=(wi, ni), device_id_type=pl.DeviceIdType.MESH)

    def x_peer(side):
        return at(w + steps[side], n)

    def y_peer(side):
        return at(w, n + steps[side])

    barrier = pltpu.get_barrier_semaphore()
    def greet(k, carry):
        @pl.when(k != w * nn + n)
        def _():
            pl.semaphore_signal(barrier, inc=1, **at(k // nn, k % nn))
        return carry

    lax.fori_loop(0, nw * nn, greet, 0)

    local = [
        pltpu.make_async_copy(stiff, kh.at[pl.ds(1, cells_x)], in_sem.at[0]),
        pltpu.make_async_copy(loads, s.at[pl.ds(0, 3), pl.ds(1, cells_x)], in_sem.at[1]),
        pltpu.make_async_copy(targets, s.at[pl.ds(3, 3), pl.ds(1, cells_x)], in_sem.at[2]),
    ]
    for copy in local:
        copy.start()

    own_state = state[0, 0]
    factor = jnp.where(own_state == 1, 1.0, jnp.where(own_state == 2, WEAK_FILL, 0.0)).astype(F32)
    act = jnp.where(factor > 0.0, 1.0, 0.0).astype(F32)
    fac_own[...] = jnp.full(fac_own.shape, factor, F32)

    pl.semaphore_wait(barrier, nw * nn - 1)

    edge = (0, cells_x - 1)
    ghost = (0, last)

    def xs_copies(side):
        there = 1 - side
        pairs = (
            (stiff.at[edge[side]], kh.at[ghost[there]]),
            (loads.at[:, edge[side]], s.at[pl.ds(0, 3), ghost[there]]),
            (targets.at[:, edge[side]], s.at[pl.ds(3, 3), ghost[there]]),
            (fac_own, fac_in.at[there]),
        )
        return [
            pltpu.make_async_remote_copy(
                src_ref=a, dst_ref=b, send_sem=xs_send.at[side, t], recv_sem=xs_recv.at[there, t],
                **x_peer(side))
            for t, (a, b) in enumerate(pairs)
        ]

    def one(src, dst, sends, recvs, side, peer):
        return pltpu.make_async_remote_copy(
            src_ref=src, dst_ref=dst, send_sem=sends.at[side], recv_sem=recvs.at[1 - side],
            **peer(side))

    def ys_copy(side):
        return one(ys_out.at[side], ys_in.at[1 - side], ys_send, ys_recv, side, y_peer)

    def yd_copy(side):
        return one(yd_out.at[side], yd_in.at[1 - side], yd_send, yd_recv, side, y_peer)

    def xd_copy(side):
        return one(d.at[:, 1 + edge[side]], d.at[:, ghost[1 - side]], xd_send, xd_recv, side, x_peer)

    def xx_copy():
        return pltpu.make_async_remote_copy(
            src_ref=s.at[:, cells_x], dst_ref=s.at[:, 0], send_sem=xx_send.at[0],
            recv_sem=xx_recv.at[0], **x_peer(1))

    def yx_copy():
        return pltpu.make_async_remote_copy(
            src_ref=yx_out, dst_ref=yx_in, send_sem=xx_send.at[1],
            recv_sem=xx_recv.at[1], **y_peer(1))

    for side in (0, 1):
        @pl.when(has_x[side])
        def _():
            for copy in xs_copies(side):
                copy.start()

        @pl.when(jnp.logical_not(has_x[side]))
        def _():
            s[:, ghost[side]] = jnp.zeros((6, cells_y, depth), F32)
            d[:, ghost[side]] = jnp.zeros((6, cells_y, depth), F32)
            fac_in[side] = jnp.zeros(fac_in.shape[1:], F32)

        @pl.when(jnp.logical_not(has_y[side]))
        def _():
            ys_in[side] = jnp.zeros(ys_in.shape[1:], F32)
            yd_in[side] = jnp.zeros(yd_in.shape[1:], F32)

    @pl.when(n == 0)
    def _():
        yx_in[...] = jnp.zeros(yx_in.shape, F32)

    for copy in local:
        copy.wait()

    half_factor = 0.5 * factor
    y_edge = (slice(0, 1), slice(cells_y - 1, cells_y))

    def prepare(t, carry):
        plane = kh[t + 1] * half_factor
        kh[t + 1] = plane
        for side in (0, 1):
            ys_out[side, 6, pl.ds(t, 1)] = plane[y_edge[side]]
            for c in range(6):
                ys_out[side, c, pl.ds(t, 1)] = s[c, t + 1, y_edge[side]] * act
        return carry

    lax.fori_loop(0, cells_x, prepare, 0)

    for side in (0, 1):
        @pl.when(has_y[side])
        def _():
            ys_copy(side).start()

    for side in (0, 1):
        @pl.when(has_y[side])
        def _():
            ys_copy(1 - side).wait_recv()

    row = lax.broadcasted_iota(jnp.int32, (cells_y, depth), 0)
    lane = lax.broadcasted_iota(jnp.int32, (cells_y, depth), 1)
    first_row, last_row = row == 0, row == cells_y - 1
    first_lane, last_lane = lane == 0, lane == depth - 1

    def down(v, halo):
        return jnp.where(first_row, halo, pltpu.roll(v, 1, 0))

    def up(v, halo):
        return jnp.where(last_row, halo, pltpu.roll(v, cells_y - 1, 0))

    def left(v):
        return pltpu.roll(v, 1, 1)

    def right(v):
        return pltpu.roll(v, depth - 1, 1)

    def y_stiff(kc, side, t):
        halo = ys_in[side, 6, pl.ds(t, 1)]
        return jnp.where(halo > 0.0, halo, kc[y_edge[side]])

    def operator(src, y_in, i, emit):
        t = i - 1
        kc = kh[i]
        fxm, fxp = kc + kh[i - 1], kc + kh[i + 1]
        fym = kc + down(kc, y_stiff(kc, 0, t))
        fyp = kc + up(kc, y_stiff(kc, 1, t))
        fzm = kc + jnp.where(first_lane, kc, left(kc))
        fzp = kc + jnp.where(last_lane, kc, right(kc))
        sums = (fxm + fxp, fym + fyp, fzm + fzp)
        total = kc + (sums[0] + sums[1] + sums[2])
        diag = [total + part for part in sums]
        fzm = jnp.where(first_lane, 0.0, fzm)
        fzp = jnp.where(last_lane, 0.0, fzp)
        for c in range(6):
            v = src[c, i]
            ax = fxm * src[c, i - 1] + fxp * src[c, i + 1]
            ay = fym * down(v, y_in[0, c, pl.ds(t, 1)]) + fyp * up(v, y_in[1, c, pl.ds(t, 1)])
            az = fzm * left(v) + fzp * right(v)
            mine = (ax, ay, az)[c % 3]
            emit(c, i, v, diag[c % 3] * v - ((ax + ay) + (az + mine)))

    alpha, beta, p, q, wd = sweep_constants()
    alpha_a, beta_a, p_a, wd_a = alpha * act, beta * act, p * act, wd * act

    def emit_d(c, i, v, image):
        plane = alpha_a * v - beta_a * image
        d[c, i] = plane
        for side in (0, 1):
            yd_out[side, c, pl.ds(i - 1, 1)] = plane[y_edge[side]]

    def emit_x(c, i, v, image):
        plane = p_a * s[c, i] + (q * v - wd_a * image)
        s[c, i] = plane
        yx_out[c, pl.ds(i - 1, 1)] = plane[y_edge[1]]

    def first_pass(i, carry):
        operator(s, ys_in, i, emit_d)
        return carry

    def second_pass(i, carry):
        operator(d, yd_in, i, emit_x)
        return carry

    lax.fori_loop(2, cells_x, first_pass, 0)

    for side in (0, 1):
        @pl.when(has_x[side])
        def _():
            for copy in xs_copies(1 - side):
                copy.wait_recv()
        theirs = fac_in[side][0:1]
        present = theirs > 0.0
        inner = kh[1 + edge[side]]

        @pl.when(has_x[side])
        def _():
            kh[ghost[side]] = jnp.where(present, kh[ghost[side]] * (0.5 * theirs), inner)
            for c in range(6):
                s[c, ghost[side]] = jnp.where(present, s[c, ghost[side]], 0.0)

        @pl.when(jnp.logical_not(has_x[side]))
        def _():
            kh[ghost[side]] = inner

    lax.fori_loop(0, 2, lambda t, c: first_pass(1 + t * (cells_x - 1), c), 0)

    for side in (0, 1):
        @pl.when(has_x[side])
        def _():
            xd_copy(side).start()

    for side in (0, 1):
        @pl.when(has_y[side])
        def _():
            yd_copy(side).start()

    for side in (0, 1):
        @pl.when(has_y[side])
        def _():
            yd_copy(1 - side).wait_recv()

    lax.fori_loop(2, cells_x, second_pass, 0)

    for side in (0, 1):
        @pl.when(has_x[side])
        def _():
            xd_copy(1 - side).wait_recv()

    lax.fori_loop(0, 2, lambda t, c: second_pass(1 + (1 - t) * (cells_x - 1), c), 0)

    @pl.when(has_x[1])
    def _():
        xx_copy().start()

    @pl.when(has_y[1])
    def _():
        yx_copy().start()

    @pl.when(has_y[0])
    def _():
        yx_copy().wait_recv()

    other_share = jnp.where(factor > 0.0, 1.0, 2.0).astype(F32)
    end_x = jnp.where(w == nw - 1, 2.0, 0.0).astype(F32)
    end_y = jnp.where(n == nn - 1, 2.0, 0.0).astype(F32)
    zero_plane = jnp.zeros((cells_y, depth), F32)
    zero_row = jnp.zeros((1, depth), F32)

    def products(shift, axis):
        total = None
        for c in range(3):
            (u, un), (l, ln) = shift(c), shift(c + 3)
            term = (u - un) * (l - ln)
            if c == axis:
                term = term + term
            total = term if total is None else total + term
        return total

    def face_sums(t, carry, behind=True):
        own, back, below = carry
        i = t + 1
        kc = kh[i]
        fields = [s[c, i] for c in range(6)]
        squares = [fields[c] * fields[c + 3] for c in range(3)]
        mass = squares[0] + squares[1] + squares[2]
        far_x = jnp.where(t == cells_x - 1, end_x, 0.0)
        far_y = jnp.where(last_row, end_y, 0.0)
        far_z = jnp.where(last_lane, 2.0, 0.0)
        own = own + kc * (
            mass + far_x * (mass + squares[0]) + far_y * (mass + squares[1])
            + far_z * (mass + squares[2]))
        if behind:
            px = products(lambda c: (fields[c], s[c, i - 1]), 0)
            own = own + (kc + kh[i - 1]) * px
        halo = ys_in[0, 6, pl.ds(t, 1)]
        py = products(lambda c: (fields[c], down(fields[c], yx_in[c, pl.ds(t, 1)])), 1)
        edge_weight = jnp.where(halo > 0.0, 0.0, kc[0:1])
        own = own + (kc + down(kc, edge_weight)) * py
        below = below + (other_share * halo) * py[0:1]
        pz = products(lambda c: (fields[c], jnp.where(first_lane, 0.0, left(fields[c]))), 2)
        own = own + jnp.where(first_lane, kc + kc, kc) * pz
        back = back + jnp.where(first_lane, 0.0, left(kc)) * pz
        return own, back, below

    start = face_sums(0, (zero_plane, zero_plane, zero_row), behind=False)
    own, back, below = lax.fori_loop(1, cells_x, face_sums, start)

    @pl.when(has_x[0])
    def _():
        xx_copy().wait_recv()

    px = products(lambda c: (s[c, 1], s[c, 0]), 0)
    present = fac_in[0][0:1] > 0.0
    own = own + kh[1] * jnp.where(present, 1.0, 2.0) * px
    beside = jnp.where(present, other_share * kh[0], 0.0) * px

    def fold(v):
        return jnp.sum(v, axis=0, keepdims=True)

    own_row = fold(own) + right(jnp.broadcast_to(fold(back), (8, depth)))[0:1]
    send_a[...] = jnp.concatenate(
        [own_row, fold(beside), below, jnp.zeros((5, depth), F32)], axis=0)

    me = w * nn + n

    def a_copy(k, slot):
        return pltpu.make_async_remote_copy(
            src_ref=send_a, dst_ref=tile_a.at[slot], send_sem=a_send.at[k],
            recv_sem=a_recv.at[slot], **at(k // nn, k % nn))

    def start_a(k, carry):
        @pl.when(k != me)
        def _():
            a_copy(k, me).start()
        return carry

    lax.fori_loop(0, nw * nn, start_a, 0)
    tile_a[me] = send_a[...]

    def wait_a(k, carry):
        @pl.when(k != me)
        def _():
            a_copy(k, k).wait_recv()
        return carry

    lax.fori_loop(0, nw * nn, wait_a, 0)

    wanted = order[me]
    groups_y = nn // 2
    b_row = lax.broadcasted_iota(jnp.int32, (8, depth), 0)
    b_block = lax.broadcasted_iota(jnp.int32, (8, depth), 1) // (depth // DZ)
    picked = jnp.zeros((8, depth), F32)
    for mw in range(nw):
        for mn in range(nn):
            near = ((mw // 2) * groups_y + mn // 2) * DZ
            beside_x = (((mw - 1) // 2) * groups_y + mn // 2) * DZ if mw > 0 else -DZ
            beside_y = ((mw // 2) * groups_y + (mn - 1) // 2) * DZ if mn > 0 else -DZ
            base = jnp.where(b_row == 0, near, jnp.where(b_row == 1, beside_x, beside_y))
            picked = picked + jnp.where(base + b_block == wanted, tile_a[mw * nn + mn], 0.0)
    scale = math.sqrt(4 * cells_x * cells_y * (depth // DZ))
    sens[0] = jnp.sum(picked) * (-1.0 / scale)

    for side in (0, 1):
        @pl.when(has_x[side])
        def _():
            for copy in xs_copies(side):
                copy.wait_send()
            xd_copy(side).wait_send()

        @pl.when(has_y[side])
        def _():
            ys_copy(side).wait_send()
            yd_copy(side).wait_send()

    @pl.when(has_x[1])
    def _():
        xx_copy().wait_send()

    @pl.when(has_y[1])
    def _():
        yx_copy().wait_send()

    def sent_a(k, carry):
        @pl.when(k != me)
        def _():
            a_copy(k, me).wait_send()
        return carry

    lax.fori_loop(0, nw * nn, sent_a, 0)


def write_out(fields, u_out, l_out, sems):
    cells_x = u_out.shape[1]
    copies = [
        pltpu.make_async_copy(fields.at[pl.ds(3 * k, 3), pl.ds(1, cells_x)], out, sems.at[k])
        for k, out in enumerate((u_out, l_out))
    ]
    for copy in copies:
        copy.start()
    for copy in copies:
        copy.wait()


def body(nw, nn, loads, targets, stiffness, tile_state, design_order):
    cells_x, cells_y, depth = stiffness.shape
    dma = pltpu.SemaphoreType.DMA
    vmem = pltpu.VMEM
    anywhere = pl.BlockSpec(memory_space=pl.ANY)
    smem = pl.BlockSpec(memory_space=pltpu.SMEM)
    field = (6, cells_x + 2, cells_y, depth)
    fields, sens = pl.pallas_call(
        functools.partial(kernel, nw, nn),
        out_shape=(pltpu.VMEM(field, F32), jax.ShapeDtypeStruct((1,), F32)),
        in_specs=[anywhere, anywhere, anywhere, smem, smem],
        out_specs=(pl.BlockSpec(memory_space=pltpu.VMEM), smem),
        scratch_shapes=[
            vmem(field, F32),
            vmem(field[1:], F32),
            vmem((8, depth), F32),
            vmem((2, 8, depth), F32),
            vmem((2, 7, cells_x, depth), F32),
            vmem((2, 7, cells_x, depth), F32),
            vmem((2, 6, cells_x, depth), F32),
            vmem((2, 6, cells_x, depth), F32),
            vmem((6, cells_x, depth), F32),
            vmem((6, cells_x, depth), F32),
            vmem((nw * nn, 8, depth), F32),
            vmem((8, depth), F32),
            dma((3,)),
            dma((2, 4)),
            dma((2, 4)),
            dma((2,)),
            dma((2,)),
            dma((2,)),
            dma((2,)),
            dma((2,)),
            dma((2,)),
            dma((2,)),
            dma((2,)),
            dma((nw * nn,)),
            dma((nw * nn,)),
        ],
        compiler_params=pltpu.CompilerParams(
            collective_id=0, has_side_effects=True, vmem_limit_bytes=61440 * 1024
        ),
    )(loads, targets, stiffness, tile_state, design_order)
    u, l = fields[:3, 1:-1], fields[3:, 1:-1]
    return u, l, sens


def solution(mesh):
    placed = (
        P(None, "wide", "narrow", None),
        P(None, "wide", "narrow", None),
        P("wide", "narrow", None),
        P("wide", "narrow"),
        P(),
    )
    return jax.shard_map(
        functools.partial(body, mesh.shape["wide"], mesh.shape["narrow"]),
        mesh=mesh,
        in_specs=placed,
        out_specs=(
            P(None, "wide", "narrow", None),
            P(None, "wide", "narrow", None),
            P(("wide", "narrow")),
        ),
        check_vma=False,
    )
```

```python
import functools
import math

import jax
import jax.numpy as jnp
from jax import lax
from jax.experimental import pallas as pl
from jax.experimental.pallas import tpu as pltpu
from jax.sharding import PartitionSpec as P

DZ = 4
SWEEPS = 3
WEAK_FILL = 0.25
LOW_BOUND = 0.0625
HIGH_BOUND = 34.0
F32 = jnp.float32


def chebyshev_weights(sweeps):
    center = 0.5 * (HIGH_BOUND + LOW_BOUND)
    spread = 0.5 * (HIGH_BOUND - LOW_BOUND)
    bound_ratio = center / spread
    previous = 1.0 / bound_ratio
    weights = []
    for sweep_index in range(sweeps):
        current = 1.0 / (2.0 * bound_ratio - previous)
        weights.append((current * previous, 2.0 * current / spread))
        previous = current
    return (center, weights)


def sweep_constants():
    center, weights = chebyshev_weights(SWEEPS)
    (w00, w01), (w10, w11) = weights[0], weights[1]
    alpha = w00 / center + w01
    beta = w01 / center
    p = 1.0 / center - w11 * w00 / (w01 * center)
    q = 1.0 + w10 + w11 / w01
    return alpha, beta, p, q, w11


def kernel(
    nw, nn, loads, targets, stiff, state, order, s, sens,
    d, kh, fac_own, fac_in, ys_out, ys_in, yd_out, yd_in, yx_out, yx_in,
    tile_a, send_a,
    in_sem, xs_send, xs_recv, ys_send, ys_recv, xd_send, xd_recv,
    yd_send, yd_recv, xx_send, xx_recv, a_send, a_recv,
):
    cells_x, cells_y, depth = stiff.shape
    last = cells_x + 1
    w = lax.axis_index("wide")
    n = lax.axis_index("narrow")
    has_x = (w > 0, w < nw - 1)
    has_y = (n > 0, n < nn - 1)
    steps = (-1, 1)

    def at(wi, ni):
        return dict(device_id=(wi, ni), device_id_type=pl.DeviceIdType.MESH)

    def x_peer(side):
        return at(w + steps[side], n)

    def y_peer(side):
        return at(w, n + steps[side])

    barrier = pltpu.get_barrier_semaphore()
    def greet(k, carry):
        @pl.when(k != w * nn + n)
        def _():
            pl.semaphore_signal(barrier, inc=1, **at(k // nn, k % nn))
        return carry

    lax.fori_loop(0, nw * nn, greet, 0)

    local = [
        pltpu.make_async_copy(stiff, kh.at[pl.ds(1, cells_x)], in_sem.at[0]),
        pltpu.make_async_copy(loads, s.at[pl.ds(0, 3), pl.ds(1, cells_x)], in_sem.at[1]),
        pltpu.make_async_copy(targets, s.at[pl.ds(3, 3), pl.ds(1, cells_x)], in_sem.at[2]),
    ]
    for copy in local:
        copy.start()

    own_state = state[0, 0]
    factor = jnp.where(own_state == 1, 1.0, jnp.where(own_state == 2, WEAK_FILL, 0.0)).astype(F32)
    act = jnp.where(factor > 0.0, 1.0, 0.0).astype(F32)
    fac_own[...] = jnp.full(fac_own.shape, factor, F32)

    pl.semaphore_wait(barrier, nw * nn - 1)

    edge = (0, cells_x - 1)
    ghost = (0, last)

    def xs_copies(side):
        there = 1 - side
        pairs = (
            (stiff.at[edge[side]], kh.at[ghost[there]]),
            (loads.at[:, edge[side]], s.at[pl.ds(0, 3), ghost[there]]),
            (targets.at[:, edge[side]], s.at[pl.ds(3, 3), ghost[there]]),
            (fac_own, fac_in.at[there]),
        )
        return [
            pltpu.make_async_remote_copy(
                src_ref=a, dst_ref=b, send_sem=xs_send.at[side, t], recv_sem=xs_recv.at[there, t],
                **x_peer(side))
            for t, (a, b) in enumerate(pairs)
        ]

    def one(src, dst, sends, recvs, side, peer):
        return pltpu.make_async_remote_copy(
            src_ref=src, dst_ref=dst, send_sem=sends.at[side], recv_sem=recvs.at[1 - side],
            **peer(side))

    def ys_copy(side):
        return one(ys_out.at[side], ys_in.at[1 - side], ys_send, ys_recv, side, y_peer)

    def yd_copy(side):
        return one(yd_out.at[side], yd_in.at[1 - side], yd_send, yd_recv, side, y_peer)

    def xd_copy(side):
        return one(d.at[:, 1 + edge[side]], d.at[:, ghost[1 - side]], xd_send, xd_recv, side, x_peer)

    def xx_copy():
        return pltpu.make_async_remote_copy(
            src_ref=s.at[:, cells_x], dst_ref=s.at[:, 0], send_sem=xx_send.at[0],
            recv_sem=xx_recv.at[0], **x_peer(1))

    def yx_copy():
        return pltpu.make_async_remote_copy(
            src_ref=yx_out, dst_ref=yx_in, send_sem=xx_send.at[1],
            recv_sem=xx_recv.at[1], **y_peer(1))

    for side in (0, 1):
        @pl.when(has_x[side])
        def _():
            for copy in xs_copies(side):
                copy.start()

        @pl.when(jnp.logical_not(has_x[side]))
        def _():
            s[:, ghost[side]] = jnp.zeros((6, cells_y, depth), F32)
            d[:, ghost[side]] = jnp.zeros((6, cells_y, depth), F32)
            fac_in[side] = jnp.zeros(fac_in.shape[1:], F32)

        @pl.when(jnp.logical_not(has_y[side]))
        def _():
            ys_in[side] = jnp.zeros(ys_in.shape[1:], F32)
            yd_in[side] = jnp.zeros(yd_in.shape[1:], F32)

    @pl.when(n == 0)
    def _():
        yx_in[...] = jnp.zeros(yx_in.shape, F32)

    for copy in local:
        copy.wait()

    half_factor = 0.5 * factor
    y_edge = (slice(0, 1), slice(cells_y - 1, cells_y))

    def prepare(t, carry):
        plane = kh[t + 1] * half_factor
        kh[t + 1] = plane
        for side in (0, 1):
            ys_out[side, 6, pl.ds(t, 1)] = plane[y_edge[side]]
            for c in range(6):
                ys_out[side, c, pl.ds(t, 1)] = s[c, t + 1, y_edge[side]] * act
        return carry

    lax.fori_loop(0, cells_x, prepare, 0)

    for side in (0, 1):
        @pl.when(has_y[side])
        def _():
            ys_copy(side).start()

    for side in (0, 1):
        @pl.when(has_y[side])
        def _():
            ys_copy(1 - side).wait_recv()

    row = lax.broadcasted_iota(jnp.int32, (cells_y, depth), 0)
    lane = lax.broadcasted_iota(jnp.int32, (cells_y, depth), 1)
    first_row, last_row = row == 0, row == cells_y - 1
    first_lane, last_lane = lane == 0, lane == depth - 1

    def down(v, halo):
        return jnp.where(first_row, halo, pltpu.roll(v, 1, 0))

    def up(v, halo):
        return jnp.where(last_row, halo, pltpu.roll(v, cells_y - 1, 0))

    def left(v):
        return pltpu.roll(v, 1, 1)

    def right(v):
        return pltpu.roll(v, depth - 1, 1)

    def y_stiff(kc, side, t):
        halo = ys_in[side, 6, pl.ds(t, 1)]
        return jnp.where(halo > 0.0, halo, kc[y_edge[side]])

    def operator(src, y_in, i, emit):
        t = i - 1
        kc = kh[i]
        fxm, fxp = kc + kh[i - 1], kc + kh[i + 1]
        fym = kc + down(kc, y_stiff(kc, 0, t))
        fyp = kc + up(kc, y_stiff(kc, 1, t))
        fzm = kc + jnp.where(first_lane, kc, left(kc))
        fzp = kc + jnp.where(last_lane, kc, right(kc))
        sums = (fxm + fxp, fym + fyp, fzm + fzp)
        total = kc + (sums[0] + sums[1] + sums[2])
        diag = [total + part for part in sums]
        fzm = jnp.where(first_lane, 0.0, fzm)
        fzp = jnp.where(last_lane, 0.0, fzp)
        for c in range(6):
            v = src[c, i]
            ax = fxm * src[c, i - 1] + fxp * src[c, i + 1]
            ay = fym * down(v, y_in[0, c, pl.ds(t, 1)]) + fyp * up(v, y_in[1, c, pl.ds(t, 1)])
            az = fzm * left(v) + fzp * right(v)
            mine = (ax, ay, az)[c % 3]
            emit(c, i, v, diag[c % 3] * v - ((ax + ay) + (az + mine)))

    alpha, beta, p, q, wd = sweep_constants()
    alpha_a, beta_a, p_a, wd_a = alpha * act, beta * act, p * act, wd * act

    def emit_d(c, i, v, image):
        plane = alpha_a * v - beta_a * image
        d[c, i] = plane
        for side in (0, 1):
            yd_out[side, c, pl.ds(i - 1, 1)] = plane[y_edge[side]]

    def emit_x(c, i, v, image):
        plane = p_a * s[c, i] + (q * v - wd_a * image)
        s[c, i] = plane
        yx_out[c, pl.ds(i - 1, 1)] = plane[y_edge[1]]

    def first_pass(i, carry):
        operator(s, ys_in, i, emit_d)
        return carry

    def second_pass(i, carry):
        operator(d, yd_in, i, emit_x)
        return carry

    lax.fori_loop(2, cells_x, first_pass, 0, unroll=3)

    for side in (0, 1):
        @pl.when(has_x[side])
        def _():
            for copy in xs_copies(1 - side):
                copy.wait_recv()
        theirs = fac_in[side][0:1]
        present = theirs > 0.0
        inner = kh[1 + edge[side]]

        @pl.when(has_x[side])
        def _():
            kh[ghost[side]] = jnp.where(present, kh[ghost[side]] * (0.5 * theirs), inner)
            for c in range(6):
                s[c, ghost[side]] = jnp.where(present, s[c, ghost[side]], 0.0)

        @pl.when(jnp.logical_not(has_x[side]))
        def _():
            kh[ghost[side]] = inner

        first_pass(1 + edge[side], 0)

        @pl.when(has_x[side])
        def _():
            xd_copy(side).start()

    for side in (0, 1):
        @pl.when(has_y[side])
        def _():
            yd_copy(side).start()

    for side in (0, 1):
        @pl.when(has_y[side])
        def _():
            yd_copy(1 - side).wait_recv()

    lax.fori_loop(2, cells_x, second_pass, 0, unroll=3)

    for side in (1, 0):
        @pl.when(has_x[side])
        def _():
            xd_copy(1 - side).wait_recv()
        second_pass(1 + edge[side], 0)
        if side == 1:
            @pl.when(has_x[1])
            def _():
                xx_copy().start()

    @pl.when(has_y[1])
    def _():
        yx_copy().start()

    @pl.when(has_y[0])
    def _():
        yx_copy().wait_recv()

    other_share = jnp.where(factor > 0.0, 1.0, 2.0).astype(F32)
    end_x = jnp.where(w == nw - 1, 2.0, 0.0).astype(F32)
    end_y = jnp.where(n == nn - 1, 2.0, 0.0).astype(F32)
    zero_plane = jnp.zeros((cells_y, depth), F32)
    zero_row = jnp.zeros((1, depth), F32)

    def products(shift, axis):
        total = None
        for c in range(3):
            (u, un), (l, ln) = shift(c), shift(c + 3)
            term = (u - un) * (l - ln)
            if c == axis:
                term = term + term
            total = term if total is None else total + term
        return total

    def face_sums(t, carry, behind=True):
        own, back, below = carry
        i = t + 1
        kc = kh[i]
        fields = [s[c, i] for c in range(6)]
        squares = [fields[c] * fields[c + 3] for c in range(3)]
        mass = squares[0] + squares[1] + squares[2]
        far_x = jnp.where(t == cells_x - 1, end_x, 0.0)
        far_y = jnp.where(last_row, end_y, 0.0)
        far_z = jnp.where(last_lane, 2.0, 0.0)
        own = own + kc * (
            mass + far_x * (mass + squares[0]) + far_y * (mass + squares[1])
            + far_z * (mass + squares[2]))
        if behind:
            px = products(lambda c: (fields[c], s[c, i - 1]), 0)
            own = own + (kc + kh[i - 1]) * px
        halo = ys_in[0, 6, pl.ds(t, 1)]
        py = products(lambda c: (fields[c], down(fields[c], yx_in[c, pl.ds(t, 1)])), 1)
        edge_weight = jnp.where(halo > 0.0, 0.0, kc[0:1])
        own = own + (kc + down(kc, edge_weight)) * py
        below = below + (other_share * halo) * py[0:1]
        pz = products(lambda c: (fields[c], jnp.where(first_lane, 0.0, left(fields[c]))), 2)
        own = own + jnp.where(first_lane, kc + kc, kc) * pz
        back = back + jnp.where(first_lane, 0.0, left(kc)) * pz
        return own, back, below

    start = face_sums(0, (zero_plane, zero_plane, zero_row), behind=False)
    own, back, below = lax.fori_loop(1, cells_x, face_sums, start)

    @pl.when(has_x[0])
    def _():
        xx_copy().wait_recv()

    px = products(lambda c: (s[c, 1], s[c, 0]), 0)
    present = fac_in[0][0:1] > 0.0
    own = own + kh[1] * jnp.where(present, 1.0, 2.0) * px
    beside = jnp.where(present, other_share * kh[0], 0.0) * px

    def fold(v):
        return jnp.sum(v, axis=0, keepdims=True)

    own_row = fold(own) + right(jnp.broadcast_to(fold(back), (8, depth)))[0:1]
    send_a[...] = jnp.concatenate(
        [own_row, fold(beside), below, jnp.zeros((5, depth), F32)], axis=0)

    me = w * nn + n

    def a_copy(k, slot):
        return pltpu.make_async_remote_copy(
            src_ref=send_a, dst_ref=tile_a.at[slot], send_sem=a_send.at[k],
            recv_sem=a_recv.at[slot], **at(k // nn, k % nn))

    def start_a(k, carry):
        @pl.when(k != me)
        def _():
            a_copy(k, me).start()
        return carry

    lax.fori_loop(0, nw * nn, start_a, 0)
    tile_a[me] = send_a[...]

    def wait_a(k, carry):
        @pl.when(k != me)
        def _():
            a_copy(k, k).wait_recv()
        return carry

    lax.fori_loop(0, nw * nn, wait_a, 0)

    wanted = order[me]
    groups_y = nn // 2
    b_row = lax.broadcasted_iota(jnp.int32, (8, depth), 0)
    b_block = lax.broadcasted_iota(jnp.int32, (8, depth), 1) // (depth // DZ)
    picked = jnp.zeros((8, depth), F32)
    for mw in range(nw):
        for mn in range(nn):
            near = ((mw // 2) * groups_y + mn // 2) * DZ
            beside_x = (((mw - 1) // 2) * groups_y + mn // 2) * DZ if mw > 0 else -DZ
            beside_y = ((mw // 2) * groups_y + (mn - 1) // 2) * DZ if mn > 0 else -DZ
            base = jnp.where(b_row == 0, near, jnp.where(b_row == 1, beside_x, beside_y))
            picked = picked + jnp.where(base + b_block == wanted, tile_a[mw * nn + mn], 0.0)
    scale = math.sqrt(4 * cells_x * cells_y * (depth // DZ))
    sens[0] = jnp.sum(picked) * (-1.0 / scale)

    for side in (0, 1):
        @pl.when(has_x[side])
        def _():
            for copy in xs_copies(side):
                copy.wait_send()
            xd_copy(side).wait_send()

        @pl.when(has_y[side])
        def _():
            ys_copy(side).wait_send()
            yd_copy(side).wait_send()

    @pl.when(has_x[1])
    def _():
        xx_copy().wait_send()

    @pl.when(has_y[1])
    def _():
        yx_copy().wait_send()

    def sent_a(k, carry):
        @pl.when(k != me)
        def _():
            a_copy(k, me).wait_send()
        return carry

    lax.fori_loop(0, nw * nn, sent_a, 0)


def write_out(fields, u_out, l_out, sems):
    cells_x = u_out.shape[1]
    copies = [
        pltpu.make_async_copy(fields.at[pl.ds(3 * k, 3), pl.ds(1, cells_x)], out, sems.at[k])
        for k, out in enumerate((u_out, l_out))
    ]
    for copy in copies:
        copy.start()
    for copy in copies:
        copy.wait()


def body(nw, nn, loads, targets, stiffness, tile_state, design_order):
    cells_x, cells_y, depth = stiffness.shape
    dma = pltpu.SemaphoreType.DMA
    vmem = pltpu.VMEM
    anywhere = pl.BlockSpec(memory_space=pl.ANY)
    smem = pl.BlockSpec(memory_space=pltpu.SMEM)
    field = (6, cells_x + 2, cells_y, depth)
    fields, sens = pl.pallas_call(
        functools.partial(kernel, nw, nn),
        out_shape=(pltpu.VMEM(field, F32), jax.ShapeDtypeStruct((1,), F32)),
        in_specs=[anywhere, anywhere, anywhere, smem, smem],
        out_specs=(pl.BlockSpec(memory_space=pltpu.VMEM), smem),
        scratch_shapes=[
            vmem(field, F32),
            vmem(field[1:], F32),
            vmem((8, depth), F32),
            vmem((2, 8, depth), F32),
            vmem((2, 7, cells_x, depth), F32),
            vmem((2, 7, cells_x, depth), F32),
            vmem((2, 6, cells_x, depth), F32),
            vmem((2, 6, cells_x, depth), F32),
            vmem((6, cells_x, depth), F32),
            vmem((6, cells_x, depth), F32),
            vmem((nw * nn, 8, depth), F32),
            vmem((8, depth), F32),
            dma((3,)),
            dma((2, 4)),
            dma((2, 4)),
            dma((2,)),
            dma((2,)),
            dma((2,)),
            dma((2,)),
            dma((2,)),
            dma((2,)),
            dma((2,)),
            dma((2,)),
            dma((nw * nn,)),
            dma((nw * nn,)),
        ],
        compiler_params=pltpu.CompilerParams(
            collective_id=0, has_side_effects=True, vmem_limit_bytes=61440 * 1024
        ),
    )(loads, targets, stiffness, tile_state, design_order)
    u, l = fields[:3, 1:-1], fields[3:, 1:-1]
    return u, l, sens


def solution(mesh):
    placed = (
        P(None, "wide", "narrow", None),
        P(None, "wide", "narrow", None),
        P("wide", "narrow", None),
        P("wide", "narrow"),
        P(),
    )
    return jax.shard_map(
        functools.partial(body, mesh.shape["wide"], mesh.shape["narrow"]),
        mesh=mesh,
        in_specs=placed,
        out_specs=(
            P(None, "wide", "narrow", None),
            P(None, "wide", "narrow", None),
            P(("wide", "narrow")),
        ),
        check_vma=False,
    )
```

```python
import functools
import math

import jax
import jax.numpy as jnp
from jax import lax
from jax.experimental import pallas as pl
from jax.experimental.pallas import tpu as pltpu
from jax.sharding import PartitionSpec as P

DZ = 4
SWEEPS = 3
WEAK_FILL = 0.25
LOW_BOUND = 0.0625
HIGH_BOUND = 34.0
F32 = jnp.float32


def chebyshev_weights(sweeps):
    center = 0.5 * (HIGH_BOUND + LOW_BOUND)
    spread = 0.5 * (HIGH_BOUND - LOW_BOUND)
    bound_ratio = center / spread
    previous = 1.0 / bound_ratio
    weights = []
    for sweep_index in range(sweeps):
        current = 1.0 / (2.0 * bound_ratio - previous)
        weights.append((current * previous, 2.0 * current / spread))
        previous = current
    return (center, weights)


def sweep_constants():
    center, weights = chebyshev_weights(SWEEPS)
    (w00, w01), (w10, w11) = weights[0], weights[1]
    alpha = w00 / center + w01
    beta = w01 / center
    p = 1.0 / center - w11 * w00 / (w01 * center)
    q = 1.0 + w10 + w11 / w01
    return alpha, beta, p, q, w11


def kernel(
    nw, nn, loads, targets, stiff, state, order, s, sens,
    d, kh, fac_own, fac_in, ys_out, ys_in, yd_out, yd_in, yx_out, yx_in,
    tile_a, send_a,
    in_sem, xs_send, xs_recv, ys_send, ys_recv, xd_send, xd_recv,
    yd_send, yd_recv, xx_send, xx_recv, a_send, a_recv,
):
    cells_x, cells_y, depth = stiff.shape
    last = cells_x + 1
    w = lax.axis_index("wide")
    n = lax.axis_index("narrow")
    has_x = (w > 0, w < nw - 1)
    has_y = (n > 0, n < nn - 1)
    steps = (-1, 1)

    def at(wi, ni):
        return dict(device_id=(wi, ni), device_id_type=pl.DeviceIdType.MESH)

    def x_peer(side):
        return at(w + steps[side], n)

    def y_peer(side):
        return at(w, n + steps[side])

    barrier = pltpu.get_barrier_semaphore()
    def greet(k, carry):
        @pl.when(k != w * nn + n)
        def _():
            pl.semaphore_signal(barrier, inc=1, **at(k // nn, k % nn))
        return carry

    lax.fori_loop(0, nw * nn, greet, 0)

    local = [
        pltpu.make_async_copy(stiff, kh.at[pl.ds(1, cells_x)], in_sem.at[0]),
        pltpu.make_async_copy(loads, s.at[pl.ds(0, 3), pl.ds(1, cells_x)], in_sem.at[1]),
        pltpu.make_async_copy(targets, s.at[pl.ds(3, 3), pl.ds(1, cells_x)], in_sem.at[2]),
    ]
    for copy in local:
        copy.start()

    own_state = state[0, 0]
    factor = jnp.where(own_state == 1, 1.0, jnp.where(own_state == 2, WEAK_FILL, 0.0)).astype(F32)
    act = jnp.where(factor > 0.0, 1.0, 0.0).astype(F32)
    fac_own[...] = jnp.full(fac_own.shape, factor, F32)

    pl.semaphore_wait(barrier, nw * nn - 1)

    edge = (0, cells_x - 1)
    ghost = (0, last)

    def xs_copies(side):
        there = 1 - side
        pairs = (
            (stiff.at[edge[side]], kh.at[ghost[there]]),
            (loads.at[:, edge[side]], s.at[pl.ds(0, 3), ghost[there]]),
            (targets.at[:, edge[side]], s.at[pl.ds(3, 3), ghost[there]]),
            (fac_own, fac_in.at[there]),
        )
        return [
            pltpu.make_async_remote_copy(
                src_ref=a, dst_ref=b, send_sem=xs_send.at[side, t], recv_sem=xs_recv.at[there, t],
                **x_peer(side))
            for t, (a, b) in enumerate(pairs)
        ]

    def one(src, dst, sends, recvs, side, peer):
        return pltpu.make_async_remote_copy(
            src_ref=src, dst_ref=dst, send_sem=sends.at[side], recv_sem=recvs.at[1 - side],
            **peer(side))

    def ys_copy(side):
        return one(ys_out.at[side], ys_in.at[1 - side], ys_send, ys_recv, side, y_peer)

    def yd_copy(side):
        return one(yd_out.at[side], yd_in.at[1 - side], yd_send, yd_recv, side, y_peer)

    def xd_copy(side):
        return one(d.at[:, 1 + edge[side]], d.at[:, ghost[1 - side]], xd_send, xd_recv, side, x_peer)

    def xx_copy():
        return pltpu.make_async_remote_copy(
            src_ref=s.at[:, cells_x], dst_ref=s.at[:, 0], send_sem=xx_send.at[0],
            recv_sem=xx_recv.at[0], **x_peer(1))

    def yx_copy():
        return pltpu.make_async_remote_copy(
            src_ref=yx_out, dst_ref=yx_in, send_sem=xx_send.at[1],
            recv_sem=xx_recv.at[1], **y_peer(1))

    for side in (0, 1):
        @pl.when(has_x[side])
        def _():
            for copy in xs_copies(side):
                copy.start()

        @pl.when(jnp.logical_not(has_x[side]))
        def _():
            s[:, ghost[side]] = jnp.zeros((6, cells_y, depth), F32)
            d[:, ghost[side]] = jnp.zeros((6, cells_y, depth), F32)
            fac_in[side] = jnp.zeros(fac_in.shape[1:], F32)

        @pl.when(jnp.logical_not(has_y[side]))
        def _():
            ys_in[side] = jnp.zeros(ys_in.shape[1:], F32)
            yd_in[side] = jnp.zeros(yd_in.shape[1:], F32)

    @pl.when(n == 0)
    def _():
        yx_in[...] = jnp.zeros(yx_in.shape, F32)

    for copy in local:
        copy.wait()

    half_factor = 0.5 * factor
    y_edge = (slice(0, 1), slice(cells_y - 1, cells_y))

    def prepare(t, carry):
        plane = kh[t + 1] * half_factor
        kh[t + 1] = plane
        for side in (0, 1):
            ys_out[side, 6, pl.ds(t, 1)] = plane[y_edge[side]]
            for c in range(6):
                ys_out[side, c, pl.ds(t, 1)] = s[c, t + 1, y_edge[side]] * act
        return carry

    lax.fori_loop(0, cells_x, prepare, 0)

    for side in (0, 1):
        @pl.when(has_y[side])
        def _():
            ys_copy(side).start()

    for side in (0, 1):
        @pl.when(has_y[side])
        def _():
            ys_copy(1 - side).wait_recv()

    row = lax.broadcasted_iota(jnp.int32, (cells_y, depth), 0)
    lane = lax.broadcasted_iota(jnp.int32, (cells_y, depth), 1)
    first_row, last_row = row == 0, row == cells_y - 1
    first_lane, last_lane = lane == 0, lane == depth - 1

    def down(v, halo):
        return jnp.where(first_row, halo, pltpu.roll(v, 1, 0))

    def up(v, halo):
        return jnp.where(last_row, halo, pltpu.roll(v, cells_y - 1, 0))

    def left(v):
        return pltpu.roll(v, 1, 1)

    def right(v):
        return pltpu.roll(v, depth - 1, 1)

    def y_stiff(kc, side, t):
        halo = ys_in[side, 6, pl.ds(t, 1)]
        return jnp.where(halo > 0.0, halo, kc[y_edge[side]])

    def operator(src, y_in, i, emit):
        t = i - 1
        kc = kh[i]
        fxm, fxp = kc + kh[i - 1], kc + kh[i + 1]
        fym = kc + down(kc, y_stiff(kc, 0, t))
        fyp = kc + up(kc, y_stiff(kc, 1, t))
        fzm = kc + jnp.where(first_lane, kc, left(kc))
        fzp = kc + jnp.where(last_lane, kc, right(kc))
        sums = (fxm + fxp, fym + fyp, fzm + fzp)
        total = kc + (sums[0] + sums[1] + sums[2])
        diag = [total + part for part in sums]
        fzm = jnp.where(first_lane, 0.0, fzm)
        fzp = jnp.where(last_lane, 0.0, fzp)
        for c in range(6):
            v = src[c, i]
            ax = fxm * src[c, i - 1] + fxp * src[c, i + 1]
            ay = fym * down(v, y_in[0, c, pl.ds(t, 1)]) + fyp * up(v, y_in[1, c, pl.ds(t, 1)])
            az = fzm * left(v) + fzp * right(v)
            mine = (ax, ay, az)[c % 3]
            emit(c, i, v, diag[c % 3] * v - ((ax + ay) + (az + mine)))

    alpha, beta, p, q, wd = sweep_constants()
    alpha_a, beta_a, p_a, wd_a = alpha * act, beta * act, p * act, wd * act

    def emit_d(c, i, v, image):
        plane = alpha_a * v - beta_a * image
        d[c, i] = plane
        for side in (0, 1):
            yd_out[side, c, pl.ds(i - 1, 1)] = plane[y_edge[side]]

    def emit_x(c, i, v, image):
        plane = p_a * s[c, i] + (q * v - wd_a * image)
        s[c, i] = plane
        yx_out[c, pl.ds(i - 1, 1)] = plane[y_edge[1]]

    def first_pass(i, carry):
        operator(s, ys_in, i, emit_d)
        return carry

    def second_pass(i, carry):
        operator(d, yd_in, i, emit_x)
        return carry

    lax.fori_loop(2, cells_x, first_pass, 0, unroll=3)

    for side in (0, 1):
        @pl.when(has_x[side])
        def _():
            for copy in xs_copies(1 - side):
                copy.wait_recv()
        theirs = fac_in[side][0:1]
        present = theirs > 0.0
        inner = kh[1 + edge[side]]

        @pl.when(has_x[side])
        def _():
            kh[ghost[side]] = jnp.where(present, kh[ghost[side]] * (0.5 * theirs), inner)
            for c in range(6):
                s[c, ghost[side]] = jnp.where(present, s[c, ghost[side]], 0.0)

        @pl.when(jnp.logical_not(has_x[side]))
        def _():
            kh[ghost[side]] = inner

        first_pass(1 + edge[side], 0)

        @pl.when(has_x[side])
        def _():
            xd_copy(side).start()

    for side in (0, 1):
        @pl.when(has_y[side])
        def _():
            yd_copy(side).start()

    for side in (0, 1):
        @pl.when(has_y[side])
        def _():
            yd_copy(1 - side).wait_recv()

    lax.fori_loop(2, cells_x, second_pass, 0, unroll=3)

    for side in (1, 0):
        @pl.when(has_x[side])
        def _():
            xd_copy(1 - side).wait_recv()
        second_pass(1 + edge[side], 0)
        if side == 1:
            @pl.when(has_x[1])
            def _():
                xx_copy().start()

    @pl.when(has_y[1])
    def _():
        yx_copy().start()

    @pl.when(has_y[0])
    def _():
        yx_copy().wait_recv()

    other_share = jnp.where(factor > 0.0, 1.0, 2.0).astype(F32)
    end_x = jnp.where(w == nw - 1, 2.0, 0.0).astype(F32)
    end_y = jnp.where(n == nn - 1, 2.0, 0.0).astype(F32)
    zero_plane = jnp.zeros((cells_y, depth), F32)
    zero_row = jnp.zeros((1, depth), F32)

    def products(shift, axis):
        total = None
        for c in range(3):
            (u, un), (l, ln) = shift(c), shift(c + 3)
            term = (u - un) * (l - ln)
            if c == axis:
                term = term + term
            total = term if total is None else total + term
        return total

    def face_sums(t, carry, behind=True):
        own, back, below = carry
        i = t + 1
        kc = kh[i]
        fields = [s[c, i] for c in range(6)]
        squares = [fields[c] * fields[c + 3] for c in range(3)]
        mass = squares[0] + squares[1] + squares[2]
        far_x = jnp.where(t == cells_x - 1, end_x, 0.0)
        far_y = jnp.where(last_row, end_y, 0.0)
        far_z = jnp.where(last_lane, 2.0, 0.0)
        own = own + kc * (
            mass + far_x * (mass + squares[0]) + far_y * (mass + squares[1])
            + far_z * (mass + squares[2]))
        if behind:
            px = products(lambda c: (fields[c], s[c, i - 1]), 0)
            own = own + (kc + kh[i - 1]) * px
        halo = ys_in[0, 6, pl.ds(t, 1)]
        py = products(lambda c: (fields[c], down(fields[c], yx_in[c, pl.ds(t, 1)])), 1)
        edge_weight = jnp.where(halo > 0.0, 0.0, kc[0:1])
        own = own + (kc + down(kc, edge_weight)) * py
        below = below + (other_share * halo) * py[0:1]
        pz = products(lambda c: (fields[c], jnp.where(first_lane, 0.0, left(fields[c]))), 2)
        own = own + jnp.where(first_lane, kc + kc, kc) * pz
        back = back + jnp.where(first_lane, 0.0, left(kc)) * pz
        return own, back, below

    start = face_sums(0, (zero_plane, zero_plane, zero_row), behind=False)
    start = face_sums(1, start)
    own, back, below = lax.fori_loop(2, cells_x, face_sums, start, unroll=3)

    @pl.when(has_x[0])
    def _():
        xx_copy().wait_recv()

    px = products(lambda c: (s[c, 1], s[c, 0]), 0)
    present = fac_in[0][0:1] > 0.0
    own = own + kh[1] * jnp.where(present, 1.0, 2.0) * px
    beside = jnp.where(present, other_share * kh[0], 0.0) * px

    def fold(v):
        return jnp.sum(v, axis=0, keepdims=True)

    own_row = fold(own) + right(jnp.broadcast_to(fold(back), (8, depth)))[0:1]
    send_a[...] = jnp.concatenate(
        [own_row, fold(beside), below, jnp.zeros((5, depth), F32)], axis=0)

    me = w * nn + n

    def a_copy(k, slot):
        return pltpu.make_async_remote_copy(
            src_ref=send_a, dst_ref=tile_a.at[slot], send_sem=a_send.at[k],
            recv_sem=a_recv.at[slot], **at(k // nn, k % nn))

    def start_a(k, carry):
        @pl.when(k != me)
        def _():
            a_copy(k, me).start()
        return carry

    lax.fori_loop(0, nw * nn, start_a, 0)
    tile_a[me] = send_a[...]

    def wait_a(k, carry):
        @pl.when(k != me)
        def _():
            a_copy(k, k).wait_recv()
        return carry

    lax.fori_loop(0, nw * nn, wait_a, 0)

    wanted = order[me]
    groups_y = nn // 2
    b_row = lax.broadcasted_iota(jnp.int32, (8, depth), 0)
    b_block = lax.broadcasted_iota(jnp.int32, (8, depth), 1) // (depth // DZ)
    picked = jnp.zeros((8, depth), F32)
    for mw in range(nw):
        for mn in range(nn):
            near = ((mw // 2) * groups_y + mn // 2) * DZ
            beside_x = (((mw - 1) // 2) * groups_y + mn // 2) * DZ if mw > 0 else -DZ
            beside_y = ((mw // 2) * groups_y + (mn - 1) // 2) * DZ if mn > 0 else -DZ
            base = jnp.where(b_row == 0, near, jnp.where(b_row == 1, beside_x, beside_y))
            picked = picked + jnp.where(base + b_block == wanted, tile_a[mw * nn + mn], 0.0)
    scale = math.sqrt(4 * cells_x * cells_y * (depth // DZ))
    sens[0] = jnp.sum(picked) * (-1.0 / scale)

    for side in (0, 1):
        @pl.when(has_x[side])
        def _():
            for copy in xs_copies(side):
                copy.wait_send()
            xd_copy(side).wait_send()

        @pl.when(has_y[side])
        def _():
            ys_copy(side).wait_send()
            yd_copy(side).wait_send()

    @pl.when(has_x[1])
    def _():
        xx_copy().wait_send()

    @pl.when(has_y[1])
    def _():
        yx_copy().wait_send()

    def sent_a(k, carry):
        @pl.when(k != me)
        def _():
            a_copy(k, me).wait_send()
        return carry

    lax.fori_loop(0, nw * nn, sent_a, 0)


def write_out(fields, u_out, l_out, sems):
    cells_x = u_out.shape[1]
    copies = [
        pltpu.make_async_copy(fields.at[pl.ds(3 * k, 3), pl.ds(1, cells_x)], out, sems.at[k])
        for k, out in enumerate((u_out, l_out))
    ]
    for copy in copies:
        copy.start()
    for copy in copies:
        copy.wait()


def body(nw, nn, loads, targets, stiffness, tile_state, design_order):
    cells_x, cells_y, depth = stiffness.shape
    dma = pltpu.SemaphoreType.DMA
    vmem = pltpu.VMEM
    anywhere = pl.BlockSpec(memory_space=pl.ANY)
    smem = pl.BlockSpec(memory_space=pltpu.SMEM)
    field = (6, cells_x + 2, cells_y, depth)
    fields, sens = pl.pallas_call(
        functools.partial(kernel, nw, nn),
        out_shape=(pltpu.VMEM(field, F32), jax.ShapeDtypeStruct((1,), F32)),
        in_specs=[anywhere, anywhere, anywhere, smem, smem],
        out_specs=(pl.BlockSpec(memory_space=pltpu.VMEM), smem),
        scratch_shapes=[
            vmem(field, F32),
            vmem(field[1:], F32),
            vmem((8, depth), F32),
            vmem((2, 8, depth), F32),
            vmem((2, 7, cells_x, depth), F32),
            vmem((2, 7, cells_x, depth), F32),
            vmem((2, 6, cells_x, depth), F32),
            vmem((2, 6, cells_x, depth), F32),
            vmem((6, cells_x, depth), F32),
            vmem((6, cells_x, depth), F32),
            vmem((nw * nn, 8, depth), F32),
            vmem((8, depth), F32),
            dma((3,)),
            dma((2, 4)),
            dma((2, 4)),
            dma((2,)),
            dma((2,)),
            dma((2,)),
            dma((2,)),
            dma((2,)),
            dma((2,)),
            dma((2,)),
            dma((2,)),
            dma((nw * nn,)),
            dma((nw * nn,)),
        ],
        compiler_params=pltpu.CompilerParams(
            collective_id=0, has_side_effects=True, vmem_limit_bytes=61440 * 1024
        ),
    )(loads, targets, stiffness, tile_state, design_order)
    u, l = fields[:3, 1:-1], fields[3:, 1:-1]
    return u, l, sens


def solution(mesh):
    placed = (
        P(None, "wide", "narrow", None),
        P(None, "wide", "narrow", None),
        P("wide", "narrow", None),
        P("wide", "narrow"),
        P(),
    )
    return jax.shard_map(
        functools.partial(body, mesh.shape["wide"], mesh.shape["narrow"]),
        mesh=mesh,
        in_specs=placed,
        out_specs=(
            P(None, "wide", "narrow", None),
            P(None, "wide", "narrow", None),
            P(("wide", "narrow")),
        ),
        check_vma=False,
    )
```
